512 devices in a mesh: row: 32 (over x, y, core), col: 16 (over z).
Axes of the slice: x: 4, y: 4, z: 16, core: 2. Of those that a mesh axis runs over, the one named last changes fastest.
Arguments:
- delta: bfloat16 [29568, 8192], P('row', 'col'), may hold values from -0.03125 to 0.03125
- probe: bfloat16 [8192, 256], P('col'), may hold values from -6 to 6
Outputs:
- q_basis: float32 [29568, 256], P('row')
- w_basis: float32 [8192, 256], P('col')
- core: float32 [256, 256], replicated
The draws below stay inside these ranges and needn't reach their ends.
All inputs are finite; a program needn't handle non-finite values.
Results may differ from the reference program's by a relative error of at most 0.0045.
Values may be sent and summed in bfloat16 or wider, within the bound.
A program may use at most 64 MiB of HBM per device.

```python
import math
import jax
import jax.numpy as jnp
from jax import lax

D = 8192
FF = 29568
R = 256
POWER = 2


def block_scale(own_key, extent, cuts, low, high):
    level, own = 1.0, jax.random.fold_in(own_key, 6)
    for axis_at, shards_of in cuts:
        draws = jnp.exp(jax.random.uniform(jax.random.fold_in(own, axis_at), (shards_of,), jnp.float32, low / len(cuts), high / len(cuts)))
        level = level * jnp.repeat(draws, extent[axis_at] // shards_of).reshape([-1 if axis == axis_at else 1 for axis in range(len(extent))])
    return level


def gaussian(stream_key, dims, spread, limit, pieces=(), held_as=jnp.bfloat16):
    loudness = block_scale(stream_key, dims, pieces, -0.22, 0.18) if pieces else 1.0
    values = jax.random.normal(stream_key, dims, jnp.float32) * spread * loudness
    return jnp.minimum(jnp.maximum(values, -limit), limit).astype(held_as)


def setup_inputs(seed: int = 0) -> dict:
    key_of = jax.random.split(jax.random.key(seed), 3)
    return {
        "delta": gaussian(key_of[0], (FF, D), FF ** -0.5, 0.03125, ((0, 32), (1, 16))),
        "probe": gaussian(key_of[1], (D, R), 1.0, 6.0, ((0, 16),)),
    }


def orthonormal(matrix):
    gram = jnp.dot(matrix.T.astype(jnp.float32), matrix.astype(jnp.float32), precision=lax.Precision.HIGHEST, preferred_element_type=jnp.float32)
    lower = jnp.linalg.cholesky(gram)
    basis = jax.scipy.linalg.solve_triangular(lower, matrix.T, lower=True).T
    return (basis, lower.T)

def sketch(delta, right):
    return jnp.dot(delta.astype(jnp.float32), right.astype(jnp.float32), preferred_element_type=jnp.float32)

def reference(delta, probe):
    basis, upper = orthonormal(sketch(delta, probe))
    right = None
    for step in range(POWER):
        back = jnp.dot(delta.T.astype(jnp.float32), basis.astype(jnp.bfloat16).astype(jnp.float32), preferred_element_type=jnp.float32)
        right, _ = orthonormal(back)
        basis, upper = orthonormal(sketch(delta, right.astype(jnp.bfloat16)))
    return (math.sqrt(FF) * basis, math.sqrt(D) * right, upper)
```

```python
import math

import jax
import jax.numpy as jnp
from jax import lax
from jax.experimental import pallas as pl
from jax.experimental.pallas import tpu as pltpu
from jax.sharding import PartitionSpec as P

D = 8192
FF = 29568
R = 256
POWER = 2

F32 = jnp.float32
BF16 = jnp.bfloat16
HIGHEST = lax.Precision.HIGHEST
MESH = pl.DeviceIdType.MESH

NZ = 16
NC = 16
CH = 64
ROWS = NZ * CH
COLS = D // NZ
PANEL = 64


def dot(a, b, dims):
    return lax.dot_general(a, b, (dims, ((), ())), precision=HIGHEST, preferred_element_type=F32)


def dot16(a, b):
    return jnp.dot(a, b, preferred_element_type=F32)


def split(x):
    high = x.astype(BF16)
    rest = x - high.astype(F32)
    middle = rest.astype(BF16)
    low = (rest - middle.astype(F32)).astype(BF16)
    return high, middle, low


def eliminate(block):
    groups = PANEL // 8
    t = [block[8 * g : 8 * g + 8, :] for g in range(groups)]
    sub = lax.broadcasted_iota(jnp.int32, (8, 128), 0)
    for q in range(groups):
        left = groups - q
        cols = [
            [jnp.broadcast_to(t[g][:, 8 * q + j : 8 * q + j + 1], (8, 128)) for j in range(8)]
            for g in range(q, groups)
        ]
        rows = [jnp.broadcast_to(t[q][j : j + 1, :], (8, 128)) for j in range(8)]
        lower = [[None] * 8 for _ in range(left)]
        for j in range(8):
            own = [jnp.broadcast_to(cols[0][j][m : m + 1, :], (8, 128)) for m in range(j, 8)]
            inverse = 1.0 / own[0]
            root = lax.rsqrt(own[0])
            for m in range(j + 1, 8):
                ratio = own[m - j] * inverse
                for g in range(left):
                    cols[g][m] = cols[g][m] - cols[g][j] * ratio
                rows[m] = rows[m] - rows[j] * ratio
            rows[j] = rows[j] * root
            for g in range(1, left):
                lower[g][j] = cols[g][j] * root
        for g in range(1, left):
            total = lower[g][0] * rows[0]
            for j in range(1, 8):
                total = total + lower[g][j] * rows[j]
            t[q + g] = t[q + g] - total
        done = rows[0]
        for j in range(1, 8):
            done = jnp.where(sub == j, rows[j], done)
        t[q] = done
    return jnp.concatenate(t, 0)


def factor_start(work, gram):
    at = lax.broadcasted_iota(jnp.int32, (R, R), 0)
    to = lax.broadcasted_iota(jnp.int32, (R, R), 1)
    work[:, :R] = gram[...]
    work[:, R:] = jnp.where(at == to, 1.0, 0.0).astype(F32)


def factor_panel(work, k):
    lane = lax.broadcasted_iota(jnp.int32, (PANEL, 128), 1)
    row = lax.broadcasted_iota(jnp.int32, (PANEL, 128), 0)
    wide = lax.broadcasted_iota(jnp.int32, (PANEL, R), 1)
    first = pl.multiple_of(k * PANEL, PANEL)
    panel = work[pl.ds(first, PANEL), :]
    block = pltpu.roll(panel[:, :R], R - k * PANEL, 1)[:, :128]
    block = jnp.where(lane < PANEL, block, jnp.where(lane == row + PANEL, 1.0, 0.0))
    inverse = eliminate(block)[:, PANEL : 2 * PANEL]
    upper = dot(inverse, panel, ((1,), (0,)))
    work[pl.ds(first, PANEL), :] = upper
    below = jnp.where(wide >= (k + 1) * PANEL, upper[:, :R], 0.0)
    work[...] = work[...] - dot(below, upper, ((0,), (0,)))


def lower_inverse(work):
    at = lax.broadcasted_iota(jnp.int32, (R, R), 0)
    to = lax.broadcasted_iota(jnp.int32, (R, R), 1)
    return jnp.where(at >= to, work[:, R:], 0.0)


def kernel(
    delta, delta_t, probe, q_out, w_out, core_out,
    part, full, arrived, basis, back, back_part, feature, gram, gram_part, gram_v, work, inv, xs, gz, piece,
    g_half, g_in, g_own, p_half, p_in, p_own,
    rs_send, rs_recv, ag_send, ag_recv, gz_send, gz_recv,
    c_send, c_recv, gs_send, gs_recv, ga_send, ga_recv, ps_send, ps_recv, pa_send, pa_recv,
    va_send, va_recv,
):
    r = lax.axis_index("row")
    z = lax.axis_index("col")
    chip = r // 2
    core = r % 2

    def along(step):
        return (r, lax.rem(z + step + NZ, NZ))

    def chip_at(step):
        return lax.rem(chip + step, NC)

    def device(other):
        return (2 * other + core, z)

    partner = (r + 1 - 2 * core, z)

    def block(index):
        return pl.ds(pl.multiple_of(lax.rem(index + 2 * NZ, NZ) * CH, CH), CH)

    def send(src, dst, s, v, to):
        return pltpu.make_async_remote_copy(
            src_ref=src, dst_ref=dst, send_sem=s, recv_sem=v, device_id=to, device_id_type=MESH
        )

    def each(count, f):
        def body(i, _):
            f(i)
            return 0

        lax.fori_loop(0, count, body, 0)

    def others(f):
        each(NC - 1, lambda i: f(i + 1))

    barrier = pltpu.get_barrier_semaphore()

    def greet(to):
        pl.semaphore_signal(barrier, inc=1, device_id=to, device_id_type=MESH)

    others(lambda d: greet(along(d)))
    others(lambda d: greet(device(chip_at(d))))
    greet(partner)
    pl.semaphore_wait(barrier, 2 * (NC - 1) + 1)

    def rs_copy(way, level, kind):
        sign = 1 - 2 * way
        far = 10 - 2 * level if kind == 0 else 9 - 2 * level
        hop = 2 if kind == 0 else 1
        at = (way * 4 + level - 1) * 2 + kind
        return send(
            part.at[block(z + sign * far)], arrived.at[at],
            rs_send.at[at], rs_recv.at[at], along(sign * hop),
        )

    def rs_list(level):
        return [(w, level, k) for w in (0, 1) for k in (0, 1) if (w, level, k) != (1, 1, 0)]

    def rs_send_level(level):
        for item in rs_list(level):
            rs_copy(*item).start()

    def rs_take_level(level):
        for way in (0, 1):
            sign = 1 - 2 * way
            where = block(z + sign * (8 - 2 * level))
            for item in rs_list(level):
                if item[0] == way:
                    rs_copy(*item).wait_recv()
            for item in rs_list(level):
                if item[0] == way:
                    at = (way * 4 + level - 1) * 2 + item[2]
                    part[where, :] = part[where, :] + arrived[at]

    def ag_copy(way, s, kind):
        sign = 1 - 2 * way
        at = (way * 4 + s - 1) * 2 + kind
        where = block(z - sign * 2 * (s - 1))
        return send(
            full.at[where], full.at[where], ag_send.at[at], ag_recv.at[at],
            along(sign * (2 if kind == 0 else 1)),
        )

    def ag_landing(way, s, kind):
        sign = 1 - 2 * way
        at = (way * 4 + s - 1) * 2 + kind
        where = block(z - sign * (2 * s if kind == 0 else 2 * s - 1))
        return send(
            full.at[where], full.at[where], ag_send.at[at], ag_recv.at[at],
            along(sign * (2 if kind == 0 else 1)),
        )

    def ag_do(s, f):
        for way in (0, 1):
            for kind in (0, 1):
                if (way, kind) == (1, 0):
                    pl.when(s < 4)(lambda way=way, kind=kind: f(way, s, kind))
                else:
                    f(way, s, kind)

    def gz_copy(d):
        return send(piece, gz.at[z], gz_send.at[d], gz_recv.at[z], along(d))

    def gz_landing(d):
        src = lax.rem(z + d, NZ)
        return send(piece, gz.at[src], gz_send.at[d], gz_recv.at[src], along(d))

    def rows_of(index, size):
        return pl.ds(pl.multiple_of(index * size, size), size)

    def scatter_copy(half, into, s, v, size, d):
        to = chip_at(d)
        return send(half.at[rows_of(to, size)], into.at[chip], s.at[d], v.at[chip], device(to))

    def scatter_landing(half, into, s, v, size, d):
        src = chip_at(d)
        return send(half.at[rows_of(src, size)], into.at[src], s.at[d], v.at[src], device(src))

    def gather_copy(own, into, s, v, size, d):
        to = chip_at(d)
        return send(own, into.at[rows_of(core * NC + chip, size)], s.at[d], v.at[chip], device(to))

    def gather_landing(own, into, s, v, size, d):
        src = chip_at(d)
        return send(own, into.at[rows_of(core * NC + src, size)], s.at[d], v.at[src], device(src))

    g_scatter = (g_half, g_in, gs_send, gs_recv, 8)
    p_scatter = (p_half, p_in, ps_send, ps_recv, 16)
    g_gather = (g_own, gram, ga_send, ga_recv, 8)
    v_gather = (g_own, gram_v, va_send, va_recv, 8)
    p_gather = (p_own, back, pa_send, pa_recv, 16)

    def swap_in(array, into, at, size):
        return send(
            array.at[rows_of(1 - core, size)], into, c_send.at[at], c_recv.at[at], partner
        )

    def swap_out(array, at, size):
        half = array.at[rows_of(core, size)]
        return send(half, half, c_send.at[at], c_recv.at[at], partner)

    def swap_landing(array, at, size):
        half = array.at[rows_of(1 - core, size)]
        return send(half, half, c_send.at[at], c_recv.at[at], partner)

    def total(into):
        value = into[0]
        for i in range(1, NC):
            value = value + into[i]
        return value

    first = probe[...]
    xs[:, :R] = first
    xs[:, R:] = jnp.zeros((COLS, 2 * R), BF16)

    def iteration(it, _):
        later = it > 0
        goes_on = it < POWER

        @pl.when(later)
        def _():
            value = feature[...]
            work[:, :R] = dot(value, value, ((0,), (0,)))
            piece[...] = work[rows_of(core * NC + chip, 8), :R]
            gz[z] = piece[...]
            others(lambda d: gz_copy(d).start())
            high, middle, low = split(value)
            xs[:, :R] = high
            xs[:, R : 2 * R] = middle
            xs[:, 2 * R :] = low

        def sketch_rows(i):
            rows = rows_of(i, 256)
            piece_of = delta[rows, :]
            small = dot16(piece_of, xs[:, 2 * R :]) + dot16(piece_of, xs[:, R : 2 * R])
            part[rows, :] = dot16(piece_of, xs[:, :R]) + small

        each(ROWS // 256, sketch_rows)

        rs_send_level(1)
        rs_take_level(1)
        rs_send_level(2)
        rs_take_level(2)
        rs_send_level(3)

        @pl.when(later)
        def _():
            others(lambda d: gz_landing(d).wait_recv())
            mine = total(gz)
            g_own[...] = mine
            gram_v[rows_of(core * NC + chip, 8), :] = mine
            others(lambda d: gather_copy(*v_gather, d).start())

        rs_take_level(3)
        rs_send_level(4)
        rs_take_level(4)
        full[block(z), :] = part[block(z), :]
        ag_do(1, lambda *a: ag_copy(*a).start())

        @pl.when(later)
        def _():
            others(lambda d: gather_landing(*v_gather, d).wait_recv())
            swap_out(gram_v, 2, 128).start()
            swap_landing(gram_v, 2, 128).wait_recv()
            swap_out(gram_v, 2, 128).wait_send()
            others(lambda d: gather_copy(*v_gather, d).wait_send())
            others(lambda d: gz_copy(d).wait_send())
            factor_start(work, gram_v)

        def panel(k):
            pl.when(later)(lambda: factor_panel(work, k))
            ag_do(k + 1, lambda *a: ag_landing(*a).wait_recv())

            @pl.when(k < 3)
            def _():
                ag_do(k + 2, lambda *a: ag_copy(*a).start())

        each(4, panel)
        for level in range(1, 5):
            for item in rs_list(level):
                rs_copy(*item).wait_send()
            ag_do(level, lambda *a: ag_copy(*a).wait_send())

        @pl.when(later)
        def _():
            inv[...] = lower_inverse(work)

            def normal_rows(i):
                rows = rows_of(i, 256)
                basis[rows, :] = dot(full[rows, :], inv[...], ((1,), (1,)))

            each(ROWS // 256, normal_rows)

        @pl.when(jnp.logical_not(later))
        def _():
            basis[...] = full[...]

        value = basis[...]
        gram_part[...] = dot(value, value, ((0,), (0,)))
        swap_in(gram_part, g_half, 0, 128).start()

        @pl.when(goes_on)
        def _():
            high, middle, low = split(basis[...])
            for i in range(2):
                rows = slice(256 * i, 256 * i + 256)
                piece_of = delta_t[rows, :]
                back_part[rows, :] = dot16(piece_of, high) + (
                    dot16(piece_of, middle) + dot16(piece_of, low)
                )
            swap_in(back_part, p_half, 1, 256).start()

        swap_in(gram_part, g_half, 0, 128).wait()
        g_half[...] = g_half[...] + gram_part[rows_of(core, 128), :]
        g_in[chip] = g_half[rows_of(chip, 8), :]
        others(lambda d: scatter_copy(*g_scatter, d).start())

        @pl.when(goes_on)
        def _():
            swap_in(back_part, p_half, 1, 256).wait()
            p_half[...] = p_half[...] + back_part[rows_of(core, 256), :]
            p_in[chip] = p_half[rows_of(chip, 16), :]
            others(lambda d: scatter_copy(*p_scatter, d).start())

        others(lambda d: scatter_landing(*g_scatter, d).wait_recv())
        mine = total(g_in)
        g_own[...] = mine
        gram[rows_of(core * NC + chip, 8), :] = mine
        others(lambda d: gather_copy(*g_gather, d).start())

        @pl.when(goes_on)
        def _():
            others(lambda d: scatter_landing(*p_scatter, d).wait_recv())
            mine = total(p_in)
            p_own[...] = mine
            back[rows_of(core * NC + chip, 16), :] = mine
            others(lambda d: gather_copy(*p_gather, d).start())

        others(lambda d: gather_landing(*g_gather, d).wait_recv())
        swap_out(gram, 3, 128).start()
        swap_landing(gram, 3, 128).wait_recv()
        swap_out(gram, 3, 128).wait_send()
        others(lambda d: scatter_copy(*g_scatter, d).wait_send())
        others(lambda d: gather_copy(*g_gather, d).wait_send())
        factor_start(work, gram)

        @pl.when(goes_on)
        def _():
            others(lambda d: gather_landing(*p_gather, d).wait_recv())
            swap_out(back, 4, 256).start()
            others(lambda d: scatter_copy(*p_scatter, d).wait_send())
            others(lambda d: gather_copy(*p_gather, d).wait_send())

        each(4, lambda k: factor_panel(work, k))

        @pl.when(goes_on)
        def _():
            swap_landing(back, 4, 256).wait_recv()
            swap_out(back, 4, 256).wait_send()
            feature[...] = dot(back[...], lower_inverse(work), ((1,), (1,)))

        return 0

    lax.fori_loop(0, POWER + 1, iteration, 0)

    w_out[...] = math.sqrt(D) * dot(feature[...], inv[...], ((1,), (1,)))
    last = lower_inverse(work)
    at = lax.broadcasted_iota(jnp.int32, (R, R), 0)
    to = lax.broadcasted_iota(jnp.int32, (R, R), 1)
    core_out[...] = jnp.where(at <= to, work[:, :R], 0.0)
    height = q_out.shape[0]
    for start in range(0, height, 256):
        stop = min(start + 256, height)
        rows = dot(basis[start : start + 256, :], last, ((1,), (1,)))
        q_out[start:stop, :] = math.sqrt(FF) * rows[: stop - start, :]


def local(delta, probe):
    row_count = delta.shape[0]
    padded = jnp.pad(delta, ((0, ROWS - row_count), (0, 0)))
    vmem = pl.BlockSpec(memory_space=pltpu.VMEM)

    def floats(*shape):
        return pltpu.VMEM(shape, F32)

    def sems(count):
        return pltpu.SemaphoreType.DMA((count,))

    return pl.pallas_call(
        kernel,
        out_shape=(
            jax.ShapeDtypeStruct((row_count, R), F32),
            jax.ShapeDtypeStruct((COLS, R), F32),
            jax.ShapeDtypeStruct((R, R), F32),
        ),
        in_specs=[vmem] * 3,
        out_specs=(vmem,) * 3,
        scratch_shapes=[
            floats(ROWS, R),
            floats(ROWS, R),
            floats(16, CH, R),
            floats(ROWS, R),
            floats(COLS, R),
            floats(COLS, R),
            floats(COLS, R),
            floats(R, R),
            floats(R, R),
            floats(R, R),
            floats(R, 2 * R),
            floats(R, R),
            pltpu.VMEM((COLS, 3 * R), BF16),
            floats(NZ, 8, R),
            floats(8, R),
            floats(128, R),
            floats(NC, 8, R),
            floats(8, R),
            floats(256, R),
            floats(NC, 16, R),
            floats(16, R),
        ]
        + [sems(16)] * 6
        + [sems(5)] * 2
        + [sems(16)] * 10,
        compiler_params=pltpu.CompilerParams(
            collective_id=0, has_side_effects=True, vmem_limit_bytes=48 << 20
        ),
        cost_estimate=pl.CostEstimate(flops=10**10, bytes_accessed=10**7, transcendentals=0),
        name="range_finder",
    )(padded, padded.T, probe)


def solution(mesh):
    in_specs = (P("row", "col"), P("col", None))
    out_specs = (P("row", None), P("col", None), P())
    return jax.shard_map(local, mesh=mesh, in_specs=in_specs, out_specs=out_specs, check_vma=False)
```

```python
import math

import jax
import jax.numpy as jnp
from jax import lax
from jax.experimental import pallas as pl
from jax.experimental.pallas import tpu as pltpu
from jax.sharding import PartitionSpec as P

D = 8192
FF = 29568
R = 256
POWER = 2

F32 = jnp.float32
BF16 = jnp.bfloat16
HIGHEST = lax.Precision.HIGHEST
MESH = pl.DeviceIdType.MESH

NZ = 16
NC = 16
ROWS = 928
WIDE = 1024
LANES = 128
CH = 120
COLS = D // NZ
PANEL = 64
PARTS = ((0, 32), (32, 32), (64, 32), (96, 24))
RS_AT = (8, 6, 4, 2, 0)
AG_AT = (0, 3, 6, 8)
TILES = ((0, 256), (256, 512), (512, 768), (768, ROWS))


def hops(marks):
    out = []
    for way in (0, 1):
        for level in range(len(marks) - 1):
            for hop in range(abs(marks[level] - marks[level + 1]), 0, -1):
                far = min(marks[level], marks[level + 1]) + hop
                if not (way == 1 and far == 8):
                    out += [(way, level, hop, part) for part in range(len(PARTS))]
    return out


RS_MESSAGES = hops(RS_AT)
AG_MESSAGES = hops(AG_AT)


def dot(a, b, dims):
    return lax.dot_general(a, b, (dims, ((), ())), precision=HIGHEST, preferred_element_type=F32)


def dot16(a, b):
    return jnp.dot(a, b, preferred_element_type=F32)


def split(x):
    high = x.astype(BF16)
    rest = x - high.astype(F32)
    middle = rest.astype(BF16)
    low = (rest - middle.astype(F32)).astype(BF16)
    return high, middle, low


def eliminate(block):
    groups = PANEL // 8
    t = [block[8 * g : 8 * g + 8, :] for g in range(groups)]
    sub = lax.broadcasted_iota(jnp.int32, (8, 128), 0)
    for q in range(groups):
        left = groups - q
        cols = [
            [jnp.broadcast_to(t[g][:, 8 * q + j : 8 * q + j + 1], (8, 128)) for j in range(8)]
            for g in range(q, groups)
        ]
        rows = [jnp.broadcast_to(t[q][j : j + 1, :], (8, 128)) for j in range(8)]
        lower = [[None] * 8 for _ in range(left)]
        for j in range(8):
            own = [jnp.broadcast_to(cols[0][j][m : m + 1, :], (8, 128)) for m in range(j, 8)]
            inverse = 1.0 / own[0]
            root = lax.rsqrt(own[0])
            for m in range(j + 1, 8):
                ratio = own[m - j] * inverse
                for g in range(left):
                    cols[g][m] = cols[g][m] - cols[g][j] * ratio
                rows[m] = rows[m] - rows[j] * ratio
            rows[j] = rows[j] * root
            for g in range(1, left):
                lower[g][j] = cols[g][j] * root
        for g in range(1, left):
            total = lower[g][0] * rows[0]
            for j in range(1, 8):
                total = total + lower[g][j] * rows[j]
            t[q + g] = t[q + g] - total
        done = rows[0]
        for j in range(1, 8):
            done = jnp.where(sub == j, rows[j], done)
        t[q] = done
    return jnp.concatenate(t, 0)


def factor_panel(work, upper, k):
    first = k * PANEL
    tile = first // LANES * LANES
    odd = k % 2 == 1
    lane = lax.broadcasted_iota(jnp.int32, (PANEL, LANES), 1)
    row = lax.broadcasted_iota(jnp.int32, (PANEL, LANES), 0)
    wide = lax.broadcasted_iota(jnp.int32, (PANEL, R), 1)
    panel = work[first : first + PANEL, :]
    block = panel[:, tile : tile + LANES]
    if odd:
        block = pltpu.roll(block, PANEL, 1)
    block = jnp.where(lane < PANEL, block, jnp.where(lane == row + PANEL, 1.0, 0.0))
    done = eliminate(block)
    product = dot(done[:, PANEL:], panel, ((1,), (0,)))
    upper[first : first + PANEL, :] = jnp.where(wide >= first, product, 0.0)
    placed = done if odd else pltpu.roll(done, PANEL, 1)
    inside = lane >= PANEL if odd else lane < PANEL
    pieces = [product[:, at : at + LANES] for at in range(0, R, LANES)]
    pieces[tile // LANES] = jnp.where(inside, placed, pieces[tile // LANES])
    fresh = jnp.concatenate(pieces, 1)
    if first + PANEL < R:
        start = (first + PANEL) // LANES * LANES
        left = product[:, start:]
        if start < first + PANEL:
            left = jnp.where(wide[:, start:] >= first + PANEL, left, 0.0)
        at = lax.broadcasted_iota(jnp.int32, (R - start, R), 1)
        old = jnp.where((at >= first) & (at < first + PANEL), 0.0, work[start:, :])
        work[start:, :] = old - dot(left, fresh, ((0,), (0,)))
    work[first : first + PANEL, :] = fresh


def norm(gram):
    return jnp.sqrt(gram[:1, :1])


def lower_inverse(work):
    at = lax.broadcasted_iota(jnp.int32, (R, R), 0)
    to = lax.broadcasted_iota(jnp.int32, (R, R), 1)
    return jnp.where(at >= to, work[...], 0.0)


def kernel(
    delta, probe, q_out, w_out, core_out,
    delta_t, part, full, arrived, basis, back, back_part, feature, gram, gram_part, gram_v, work, upper, inv, l_inv, gz, piece,
    g_half, g_in, g_own, p_half, p_in, p_own,
    rs_send, rs_recv, ag_send, ag_recv, gz_send, gz_recv,
    c_send, c_recv, gs_send, gs_recv, ga_send, ga_recv, ps_send, ps_recv, pa_send, pa_recv,
    va_send, va_recv,
):
    r = lax.axis_index("row")
    z = lax.axis_index("col")
    chip = r // 2
    core = r % 2

    def along(step):
        return (r, lax.rem(z + step + NZ, NZ))

    def chip_at(step):
        return lax.rem(chip + step, NC)

    def device(other):
        return (2 * other + core, z)

    partner = (r + 1 - 2 * core, z)

    def block(index, part_at):
        start, size = PARTS[part_at]
        return pl.ds(pl.multiple_of(lax.rem(index + 2 * NZ, NZ) * CH + start, 8), size)

    def send(src, dst, s, v, to):
        return pltpu.make_async_remote_copy(
            src_ref=src, dst_ref=dst, send_sem=s, recv_sem=v, device_id=to, device_id_type=MESH
        )

    def each(count, f):
        def body(i, _):
            f(i)
            return 0

        lax.fori_loop(0, count, body, 0)

    def others(f):
        for d in range(1, NC):
            f(d)

    barrier = pltpu.get_barrier_semaphore()

    def greet(to):
        pl.semaphore_signal(barrier, inc=1, device_id=to, device_id_type=MESH)

    others(lambda d: greet(along(d)))
    others(lambda d: greet(device(chip_at(d))))
    greet(partner)

    def sketch(terms):
        for start, stop in TILES:
            stop = min(stop, delta.shape[0])
            rows = delta[start:stop, :]
            value = dot16(rows, terms[-1])
            for term in terms[-2::-1]:
                value = value + dot16(rows, term)
            part[start:stop, :] = value[:, :LANES]
            part[ROWS + start : ROWS + stop, :] = value[:, LANES:]

    def turn():
        height = delta.shape[0]
        for start in range(0, WIDE, LANES):
            rows = delta[start : min(start + LANES, height), :]
            if start + LANES > height:
                rest = jnp.zeros((start + LANES - height, COLS), F32)
                rows = jnp.concatenate([rows.astype(F32), rest], 0).astype(BF16)
            delta_t[:, start : start + LANES] = rows.T

    for at in (ROWS - 8, 2 * ROWS - 8):
        part[at : at + 8, :] = jnp.zeros((8, LANES), F32)
    part[2 * ROWS :, :] = jnp.zeros((NZ * CH - 2 * ROWS, LANES), F32)
    basis[ROWS:, :] = jnp.zeros((WIDE - ROWS, R), F32)
    sketch([probe[...]])
    pl.semaphore_wait(barrier, 2 * (NC - 1) + 1)

    def sign(way, p):
        return 1 - 2 * ((way + p) % 2)

    def rs_copy(way, level, hop, p):
        at = RS_MESSAGES.index((way, level, hop, p))
        to = sign(way, p)
        return send(
            part.at[block(z + to * (RS_AT[level + 1] + hop), p)],
            arrived.at[at, pl.ds(0, PARTS[p][1])],
            rs_send.at[at], rs_recv.at[at], along(to * hop),
        )

    def rs_start(level, p):
        for item in RS_MESSAGES:
            if item[1] == level and item[3] == p:
                rs_copy(*item).start()

    def rs_take(level, p):
        for way in (0, 1):
            where = block(z + sign(way, p) * RS_AT[level + 1], p)
            value = part[where, :]
            items = [m for m in RS_MESSAGES if (m[0], m[1], m[3]) == (way, level, p)]
            for item in items:
                rs_copy(*item).wait_recv()
            for item in items:
                value = value + arrived[RS_MESSAGES.index(item), : PARTS[p][1], :]
            part[where, :] = value

    def ag_copy(way, level, hop, p, landing=False):
        at = AG_MESSAGES.index((way, level, hop, p))
        to = sign(way, p)
        where = block(z - to * (AG_AT[level] + (hop if landing else 0)), p)
        return send(
            full.at[where], full.at[where], ag_send.at[at], ag_recv.at[at], along(to * hop)
        )

    def ag_start(level, p):
        for item in AG_MESSAGES:
            if item[1] == level and item[3] == p:
                ag_copy(*item).start()

    def ag_take(level, p):
        for item in AG_MESSAGES:
            if item[1] == level and item[3] == p:
                ag_copy(*item, landing=True).wait_recv()

    def gz_copy(d):
        return send(piece, gz.at[z], gz_send.at[d], gz_recv.at[z], along(d))

    def gz_landing(d):
        src = lax.rem(z + d, NZ)
        return send(piece, gz.at[src], gz_send.at[d], gz_recv.at[src], along(d))

    def rows_of(index, size):
        return pl.ds(pl.multiple_of(index * size, size), size)

    def scatter_copy(half, into, s, v, size, d):
        to = chip_at(d)
        return send(half.at[rows_of(to, size)], into.at[chip], s.at[d], v.at[chip], device(to))

    def scatter_landing(half, into, s, v, size, d):
        src = chip_at(d)
        return send(half.at[rows_of(src, size)], into.at[src], s.at[d], v.at[src], device(src))

    def gather_copy(own, into, s, v, size, d):
        to = chip_at(d)
        return send(own, into.at[rows_of(core * NC + chip, size)], s.at[d], v.at[chip], device(to))

    def gather_landing(own, into, s, v, size, d):
        src = chip_at(d)
        return send(own, into.at[rows_of(core * NC + src, size)], s.at[d], v.at[src], device(src))

    g_scatter = (g_half, g_in, gs_send, gs_recv, 8)
    p_scatter = (p_half, p_in, ps_send, ps_recv, 16)
    g_gather = (g_own, gram, ga_send, ga_recv, 8)
    v_gather = (g_own, gram_v, va_send, va_recv, 8)
    p_gather = (p_own, back, pa_send, pa_recv, 16)

    def swap_in(array, into, at, size):
        return send(
            array.at[rows_of(1 - core, size)], into, c_send.at[at], c_recv.at[at], partner
        )

    def swap_out(array, at, size):
        half = array.at[rows_of(core, size)]
        return send(half, half, c_send.at[at], c_recv.at[at], partner)

    def swap_landing(array, at, size):
        half = array.at[rows_of(1 - core, size)]
        return send(half, half, c_send.at[at], c_recv.at[at], partner)

    def total(into):
        value = into[0]
        for i in range(1, NC):
            value = value + into[i]
        return value

    def iteration(it, _):
        later = it > 0
        goes_on = it < POWER
        count = range(len(PARTS))

        for p in count:
            rs_start(0, p)

        @pl.when(later)
        def _():
            factor_panel(work, upper, 2)

        for p in count:
            rs_take(0, p)
            rs_start(1, p)

        @pl.when(later)
        def _():
            factor_panel(work, upper, 3)
            l_inv[...] = lower_inverse(work)
            value = dot(back[...], l_inv[...], ((1,), (1,)))
            feature[...] = value
            gram_part[...] = dot(value, value, ((0,), (0,)))
            piece[...] = gram_part[rows_of(core * NC + chip, 8), :]
            gz[z] = piece[...]
            others(lambda d: gz_copy(d).start())

        @pl.when(jnp.logical_not(later))
        def _():
            turn()

        for level in (1, 2):
            for p in count:
                rs_take(level, p)
                rs_start(level + 1, p)

        @pl.when(later)
        def _():
            others(lambda d: gz_landing(d).wait_recv())
            mine = total(gz)
            g_own[...] = mine
            gram_v[rows_of(core * NC + chip, 8), :] = mine
            others(lambda d: gather_copy(*v_gather, d).start())

        for p in count:
            rs_take(3, p)
            full[block(z, p), :] = part[block(z, p), :]
            ag_start(0, p)
        for p in count:
            ag_take(0, p)
            ag_start(1, p)

        @pl.when(later)
        def _():
            others(lambda d: gather_landing(*v_gather, d).wait_recv())
            swap_out(gram_v, 2, 128).start()
            others(lambda d: gather_copy(*v_gather, d).wait_send())
            others(lambda d: gz_copy(d).wait_send())
            swap_landing(gram_v, 2, 128).wait_recv()
            swap_out(gram_v, 2, 128).wait_send()
            work[...] = gram_v[...]
            factor_panel(work, upper, 0)

        for p in count:
            ag_take(1, p)
            ag_start(2, p)

        @pl.when(later)
        def _():
            for k in range(1, R // PANEL):
                factor_panel(work, upper, k)
            inv[...] = lower_inverse(work)
            l_inv[...] = norm(gram) * dot(inv[...], l_inv[...], ((1,), (0,)))

        for p in count:
            ag_take(2, p)

        def sketch_rows(start, stop):
            return jnp.concatenate(
                [full[start:stop, :], full[ROWS + start : ROWS + stop, :]], 1
            )

        @pl.when(later)
        def _():
            for start, stop in TILES:
                basis[start:stop, :] = dot(sketch_rows(start, stop), l_inv[...], ((1,), (1,)))

        @pl.when(jnp.logical_not(later))
        def _():
            for start, stop in TILES:
                basis[start:stop, :] = sketch_rows(start, stop)

        value = basis[:ROWS, :]
        gram_part[...] = dot(value, value, ((0,), (0,)))
        swap_in(gram_part, g_half, 0, 128).start()

        @pl.when(goes_on)
        def _():
            high, middle, low = split(basis[...])
            for i in range(2):
                rows = slice(256 * i, 256 * i + 256)
                piece_of = delta_t[rows, :]
                back_part[rows, :] = dot16(piece_of, high) + (
                    dot16(piece_of, middle) + dot16(piece_of, low)
                )
            swap_in(back_part, p_half, 1, 256).start()

        swap_in(gram_part, g_half, 0, 128).wait()
        g_half[...] = g_half[...] + gram_part[rows_of(core, 128), :]
        g_in[chip] = g_half[rows_of(chip, 8), :]
        others(lambda d: scatter_copy(*g_scatter, d).start())

        @pl.when(goes_on)
        def _():
            swap_in(back_part, p_half, 1, 256).wait()
            p_half[...] = p_half[...] + back_part[rows_of(core, 256), :]
            p_in[chip] = p_half[rows_of(chip, 16), :]
            others(lambda d: scatter_copy(*p_scatter, d).start())

        for item in RS_MESSAGES:
            rs_copy(*item).wait_send()
        for item in AG_MESSAGES:
            ag_copy(*item).wait_send()
        others(lambda d: scatter_landing(*g_scatter, d).wait_recv())
        mine = total(g_in)
        g_own[...] = mine
        gram[rows_of(core * NC + chip, 8), :] = mine
        others(lambda d: gather_copy(*g_gather, d).start())

        @pl.when(goes_on)
        def _():
            others(lambda d: scatter_landing(*p_scatter, d).wait_recv())
            mine = total(p_in)
            p_own[...] = mine
            back[rows_of(core * NC + chip, 16), :] = mine
            others(lambda d: gather_copy(*p_gather, d).start())

        others(lambda d: gather_landing(*g_gather, d).wait_recv())
        swap_out(gram, 3, 128).start()
        swap_landing(gram, 3, 128).wait_recv()
        swap_out(gram, 3, 128).wait_send()
        others(lambda d: scatter_copy(*g_scatter, d).wait_send())
        others(lambda d: gather_copy(*g_gather, d).wait_send())
        work[...] = gram[...]
        factor_panel(work, upper, 0)

        @pl.when(goes_on)
        def _():
            others(lambda d: gather_landing(*p_gather, d).wait_recv())
            swap_out(back, 4, 256).start()
            others(lambda d: scatter_copy(*p_scatter, d).wait_send())
            others(lambda d: gather_copy(*p_gather, d).wait_send())

        factor_panel(work, upper, 1)

        @pl.when(goes_on)
        def _():
            swap_landing(back, 4, 256).wait_recv()
            swap_out(back, 4, 256).wait_send()
            sketch(split(back[...] * (1.0 / norm(gram))))

        return 0

    lax.fori_loop(0, POWER + 1, iteration, 0)

    for k in range(2, R // PANEL):
        factor_panel(work, upper, k)

    w_out[...] = math.sqrt(D) * dot(feature[...], inv[...], ((1,), (1,)))
    last = lower_inverse(work)
    at = lax.broadcasted_iota(jnp.int32, (R, R), 0)
    to = lax.broadcasted_iota(jnp.int32, (R, R), 1)
    core_out[...] = jnp.where(at <= to, upper[...], 0.0)
    height = q_out.shape[0]
    for start in range(0, height, 256):
        stop = min(start + 256, height)
        rows = dot(basis[start : start + 256, :], last, ((1,), (1,)))
        q_out[start:stop, :] = math.sqrt(FF) * rows[: stop - start, :]


def local(delta, probe):
    row_count = delta.shape[0]
    vmem = pl.BlockSpec(memory_space=pltpu.VMEM)

    def floats(*shape):
        return pltpu.VMEM(shape, F32)

    def sems(count):
        return pltpu.SemaphoreType.DMA((count,))

    return pl.pallas_call(
        kernel,
        out_shape=(
            jax.ShapeDtypeStruct((row_count, R), F32),
            jax.ShapeDtypeStruct((COLS, R), F32),
            jax.ShapeDtypeStruct((R, R), F32),
        ),
        in_specs=[vmem] * 2,
        out_specs=(vmem,) * 3,
        scratch_shapes=[
            pltpu.VMEM((COLS, WIDE), BF16),
            floats(NZ * CH, LANES),
            floats(NZ * CH, LANES),
            floats(len(RS_MESSAGES), PARTS[0][1], LANES),
            floats(WIDE, R),
            floats(COLS, R),
            floats(COLS, R),
            floats(COLS, R),
            floats(R, R),
            floats(R, R),
            floats(R, R),
            floats(R, R),
            floats(R, R),
            floats(R, R),
            floats(R, R),
            floats(NZ, 8, R),
            floats(8, R),
            floats(128, R),
            floats(NC, 8, R),
            floats(8, R),
            floats(256, R),
            floats(NC, 16, R),
            floats(16, R),
        ]
        + [sems(len(RS_MESSAGES))] * 2
        + [sems(len(AG_MESSAGES))] * 2
        + [sems(16)] * 2
        + [sems(5)] * 2
        + [sems(16)] * 10,
        compiler_params=pltpu.CompilerParams(
            collective_id=0, has_side_effects=True, vmem_limit_bytes=48 << 20
        ),
        cost_estimate=pl.CostEstimate(flops=10**10, bytes_accessed=10**7, transcendentals=0),
        name="range_finder",
    )(delta, probe)


def solution(mesh):
    in_specs = (P("row", "col"), P("col", None))
    out_specs = (P("row", None), P("col", None), P())
    return jax.shard_map(local, mesh=mesh, in_specs=in_specs, out_specs=out_specs, check_vma=False)
```

```python
import math

import jax
import jax.numpy as jnp
from jax import lax
from jax.experimental import pallas as pl
from jax.experimental.pallas import tpu as pltpu
from jax.sharding import PartitionSpec as P

D = 8192
FF = 29568
R = 256
POWER = 2

F32 = jnp.float32
BF16 = jnp.bfloat16
HIGHEST = lax.Precision.HIGHEST
MESH = pl.DeviceIdType.MESH

NZ = 16
NC = 16
ROWS = 928
WIDE = 1024
LANES = 128
CH = 120
COLS = D // NZ
PANEL = 64
PARTS = ((0, 32), (32, 32), (64, 32), (96, 24))
RS_AT = (8, 6, 4, 2, 0)
AG_AT = (0, 2, 5, 8)
TILES = ((0, 256), (256, 512), (512, 768), (768, ROWS))

PLANE_ORDER = (10, 6, 14, 9, 11, 2, 8, 5, 7, 13, 15, 1, 3, 4, 12)
LINE_ORDER = (8, 7, 9, 6, 10, 5, 11, 4, 12, 3, 13, 2, 14, 1, 15)


def hops(marks):
    out = []
    for way in (0, 1):
        for level in range(len(marks) - 1):
            for hop in range(abs(marks[level] - marks[level + 1]), 0, -1):
                far = min(marks[level], marks[level + 1]) + hop
                if not (way == 1 and far == 8):
                    out += [(way, level, hop, part) for part in range(len(PARTS))]
    return out


RS_MESSAGES = hops(RS_AT)
AG_MESSAGES = hops(AG_AT)


def dot(a, b, dims):
    return lax.dot_general(a, b, (dims, ((), ())), precision=HIGHEST, preferred_element_type=F32)


def dot16(a, b):
    return jnp.dot(a, b, preferred_element_type=F32)


def split(x):
    high = x.astype(BF16)
    return high, (x - high.astype(F32)).astype(BF16)


def dot_t(a, b):
    def part(x, y):
        return lax.dot_general(x, y, (((1,), (1,)), ((), ())), preferred_element_type=F32)

    a_high, a_low = split(a)
    b_high, b_low = b
    return part(a_high, b_high) + (part(a_high, b_low) + part(a_low, b_high))


def eliminate(block):
    groups = PANEL // 8
    t = [block[8 * g : 8 * g + 8, :] for g in range(groups)]
    sub = lax.broadcasted_iota(jnp.int32, (8, 128), 0)
    for q in range(groups):
        left = groups - q
        cols = [
            [jnp.broadcast_to(t[g][:, 8 * q + j : 8 * q + j + 1], (8, 128)) for j in range(8)]
            for g in range(q, groups)
        ]
        rows = [jnp.broadcast_to(t[q][j : j + 1, :], (8, 128)) for j in range(8)]
        lower = [[None] * 8 for _ in range(left)]
        for j in range(8):
            own = [jnp.broadcast_to(cols[0][j][m : m + 1, :], (8, 128)) for m in range(j, 8)]
            inverse = 1.0 / own[0]
            root = lax.rsqrt(own[0])
            for m in range(j + 1, 8):
                ratio = own[m - j] * inverse
                for g in range(left):
                    cols[g][m] = cols[g][m] - cols[g][j] * ratio
                rows[m] = rows[m] - rows[j] * ratio
            rows[j] = rows[j] * root
            for g in range(1, left):
                lower[g][j] = cols[g][j] * root
        for g in range(1, left):
            total = lower[g][0] * rows[0]
            for j in range(1, 8):
                total = total + lower[g][j] * rows[j]
            t[q + g] = t[q + g] - total
        done = rows[0]
        for j in range(1, 8):
            done = jnp.where(sub == j, rows[j], done)
        t[q] = done
    return jnp.concatenate(t, 0)


def factor_panel(work, upper, k):
    first = k * PANEL
    tile = first // LANES * LANES
    odd = k % 2 == 1
    lane = lax.broadcasted_iota(jnp.int32, (PANEL, LANES), 1)
    row = lax.broadcasted_iota(jnp.int32, (PANEL, LANES), 0)
    wide = lax.broadcasted_iota(jnp.int32, (PANEL, R), 1)
    panel = work[first : first + PANEL, :]
    block = panel[:, tile : tile + LANES]
    if odd:
        block = pltpu.roll(block, PANEL, 1)
    block = jnp.where(lane < PANEL, block, jnp.where(lane == row + PANEL, 1.0, 0.0))
    done = eliminate(block)
    product = dot(done[:, PANEL:], panel, ((1,), (0,)))
    upper[first : first + PANEL, :] = jnp.where(wide >= first, product, 0.0)
    placed = done if odd else pltpu.roll(done, PANEL, 1)
    inside = lane >= PANEL if odd else lane < PANEL
    pieces = [product[:, at : at + LANES] for at in range(0, R, LANES)]
    pieces[tile // LANES] = jnp.where(inside, placed, pieces[tile // LANES])
    fresh = jnp.concatenate(pieces, 1)
    if first + PANEL < R:
        start = (first + PANEL) // LANES * LANES
        left = product[:, start:]
        if start < first + PANEL:
            left = jnp.where(wide[:, start:] >= first + PANEL, left, 0.0)
        at = lax.broadcasted_iota(jnp.int32, (R - start, R), 1)
        old = jnp.where((at >= first) & (at < first + PANEL), 0.0, work[start:, :])
        work[start:, :] = old - dot(left, fresh, ((0,), (0,)))
    work[first : first + PANEL, :] = fresh


def norm(gram):
    return jnp.sqrt(gram[:1, :1])


def lower_inverse(work):
    at = lax.broadcasted_iota(jnp.int32, (R, R), 0)
    to = lax.broadcasted_iota(jnp.int32, (R, R), 1)
    return jnp.where(at >= to, work[...], 0.0)


def kernel(
    delta, probe, q_out, w_out, core_out,
    delta_t, part, full, arrived, basis, back, back_part, feature, gram, gram_part, gram_v, work, upper, inv, l_inv, gz, piece,
    g_half, g_in, g_own, p_half, p_in, p_own,
    rs_send, rs_recv, ag_send, ag_recv, gz_send, gz_recv,
    c_send, c_recv, gs_send, gs_recv, ga_send, ga_recv, ps_send, ps_recv, pa_send, pa_recv,
    va_send, va_recv,
):
    r = lax.axis_index("row")
    z = lax.axis_index("col")
    chip = r // 2
    core = r % 2

    def along(step):
        return (r, lax.rem(z + step + NZ, NZ))

    def chip_at(step):
        return lax.rem(chip + step, NC)

    def device(other):
        return (2 * other + core, z)

    partner = (r + 1 - 2 * core, z)

    def block(index, part_at):
        start, size = PARTS[part_at]
        return pl.ds(pl.multiple_of(lax.rem(index + 2 * NZ, NZ) * CH + start, 8), size)

    def send(src, dst, s, v, to):
        return pltpu.make_async_remote_copy(
            src_ref=src, dst_ref=dst, send_sem=s, recv_sem=v, device_id=to, device_id_type=MESH
        )

    def each(count, f):
        def body(i, _):
            f(i)
            return 0

        lax.fori_loop(0, count, body, 0)

    def others(f, order=PLANE_ORDER):
        for d in order:
            f(d)

    barrier = pltpu.get_barrier_semaphore()

    def greet(to):
        pl.semaphore_signal(barrier, inc=1, device_id=to, device_id_type=MESH)

    others(lambda d: greet(along(d)))
    others(lambda d: greet(device(chip_at(d))))
    greet(partner)

    def sketch(terms):
        for start, stop in TILES:
            stop = min(stop, delta.shape[0])
            rows = delta[start:stop, :]
            value = dot16(rows, terms[-1])
            for term in terms[-2::-1]:
                value = value + dot16(rows, term)
            part[start:stop, :] = value[:, :LANES]
            part[ROWS + start : ROWS + stop, :] = value[:, LANES:]

    def turn():
        height = delta.shape[0]
        for start in range(0, WIDE, LANES):
            rows = delta[start : min(start + LANES, height), :]
            if start + LANES > height:
                rest = jnp.zeros((start + LANES - height, COLS), F32)
                rows = jnp.concatenate([rows.astype(F32), rest], 0).astype(BF16)
            delta_t[:, start : start + LANES] = rows.T

    for at in (ROWS - 8, 2 * ROWS - 8):
        part[at : at + 8, :] = jnp.zeros((8, LANES), F32)
    part[2 * ROWS :, :] = jnp.zeros((NZ * CH - 2 * ROWS, LANES), F32)
    basis[ROWS:, :] = jnp.zeros((WIDE - ROWS, R), F32)
    sketch([probe[...]])
    pl.semaphore_wait(barrier, 2 * (NC - 1) + 1)

    def sign(way, p):
        return 1 - 2 * ((way + p) % 2)

    def rs_copy(way, level, hop, p):
        at = RS_MESSAGES.index((way, level, hop, p))
        to = sign(way, p)
        return send(
            part.at[block(z + to * (RS_AT[level + 1] + hop), p)],
            arrived.at[at, pl.ds(0, PARTS[p][1])],
            rs_send.at[at], rs_recv.at[at], along(to * hop),
        )

    def rs_start(level, p):
        for item in RS_MESSAGES:
            if item[1] == level and item[3] == p:
                rs_copy(*item).start()

    def rs_take(level, p):
        for way in (0, 1):
            where = block(z + sign(way, p) * RS_AT[level + 1], p)
            value = part[where, :]
            items = [m for m in RS_MESSAGES if (m[0], m[1], m[3]) == (way, level, p)]
            for item in items:
                rs_copy(*item).wait_recv()
            for item in items:
                value = value + arrived[RS_MESSAGES.index(item), : PARTS[p][1], :]
            part[where, :] = value

    def ag_copy(way, level, hop, p, landing=False):
        at = AG_MESSAGES.index((way, level, hop, p))
        to = sign(way, p)
        where = block(z - to * (AG_AT[level] + (hop if landing else 0)), p)
        return send(
            full.at[where], full.at[where], ag_send.at[at], ag_recv.at[at], along(to * hop)
        )

    def ag_start(level, p):
        for item in AG_MESSAGES:
            if item[1] == level and item[3] == p:
                ag_copy(*item).start()

    def ag_take(level, p):
        for item in AG_MESSAGES:
            if item[1] == level and item[3] == p:
                ag_copy(*item, landing=True).wait_recv()

    def gz_copy(d):
        return send(piece, gz.at[z], gz_send.at[d], gz_recv.at[z], along(d))

    def gz_landing(d):
        src = lax.rem(z + d, NZ)
        return send(piece, gz.at[src], gz_send.at[d], gz_recv.at[src], along(d))

    def rows_of(index, size):
        return pl.ds(pl.multiple_of(index * size, size), size)

    def scatter_copy(half, into, s, v, size, d):
        to = chip_at(d)
        return send(half.at[rows_of(to, size)], into.at[chip], s.at[d], v.at[chip], device(to))

    def scatter_landing(half, into, s, v, size, d):
        src = chip_at(d)
        return send(half.at[rows_of(src, size)], into.at[src], s.at[d], v.at[src], device(src))

    def gather_copy(own, into, s, v, size, d):
        to = chip_at(d)
        return send(own, into.at[rows_of(core * NC + chip, size)], s.at[d], v.at[chip], device(to))

    def gather_landing(own, into, s, v, size, d):
        src = chip_at(d)
        return send(own, into.at[rows_of(core * NC + src, size)], s.at[d], v.at[src], device(src))

    g_scatter = (g_half, g_in, gs_send, gs_recv, 8)
    p_scatter = (p_half, p_in, ps_send, ps_recv, 16)
    g_gather = (g_own, gram, ga_send, ga_recv, 8)
    v_gather = (g_own, gram_v, va_send, va_recv, 8)
    p_gather = (p_own, back, pa_send, pa_recv, 16)

    def swap_in(array, into, at, size):
        return send(
            array.at[rows_of(1 - core, size)], into, c_send.at[at], c_recv.at[at], partner
        )

    def swap_out(array, at, size):
        half = array.at[rows_of(core, size)]
        return send(half, half, c_send.at[at], c_recv.at[at], partner)

    def swap_landing(array, at, size):
        half = array.at[rows_of(1 - core, size)]
        return send(half, half, c_send.at[at], c_recv.at[at], partner)

    def total(into):
        value = into[0]
        for i in range(1, NC):
            value = value + into[i]
        return value

    def iteration(it, _):
        later = it > 0
        goes_on = it < POWER
        count = range(len(PARTS))

        for p in count:
            rs_start(0, p)

        @pl.when(later)
        def _():
            factor_panel(work, upper, 2)

        for p in count:
            rs_take(0, p)
            rs_start(1, p)

        @pl.when(later)
        def _():
            factor_panel(work, upper, 3)
            l_inv[...] = lower_inverse(work)
            value = dot_t(back[...], split(l_inv[...]))
            feature[...] = value
            gram_part[...] = dot(value, value, ((0,), (0,)))
            piece[...] = gram_part[rows_of(core * NC + chip, 8), :]
            gz[z] = piece[...]
            others(lambda d: gz_copy(d).start(), LINE_ORDER)

        @pl.when(jnp.logical_not(later))
        def _():
            turn()

        for level in range(1, len(RS_AT) - 2):
            for p in count:
                rs_take(level, p)
                rs_start(level + 1, p)

        for p in count:
            rs_take(len(RS_AT) - 2, p)
            full[block(z, p), :] = part[block(z, p), :]
            ag_start(0, p)
        @pl.when(later)
        def _():
            others(lambda d: gz_landing(d).wait_recv())
            mine = total(gz)
            g_own[...] = mine
            gram_v[rows_of(core * NC + chip, 8), :] = mine
            others(lambda d: gather_copy(*v_gather, d).start())

        for p in count:
            ag_take(0, p)
            ag_start(1, p)

        @pl.when(later)
        def _():
            others(lambda d: gather_landing(*v_gather, d).wait_recv())
            swap_out(gram_v, 2, 128).start()
            others(lambda d: gather_copy(*v_gather, d).wait_send())
            others(lambda d: gz_copy(d).wait_send())
            swap_landing(gram_v, 2, 128).wait_recv()
            swap_out(gram_v, 2, 128).wait_send()
            work[...] = gram_v[...]
            factor_panel(work, upper, 0)

        for p in count:
            ag_take(1, p)
            ag_start(2, p)

        @pl.when(later)
        def _():
            for k in range(1, R // PANEL):
                factor_panel(work, upper, k)
            inv[...] = lower_inverse(work)
            l_inv[...] = norm(gram) * dot(inv[...], l_inv[...], ((1,), (0,)))

        for p in count:
            ag_take(2, p)

        def sketch_rows(start, stop):
            return jnp.concatenate(
                [full[start:stop, :], full[ROWS + start : ROWS + stop, :]], 1
            )

        @pl.when(later)
        def _():
            terms = split(l_inv[...])
            for start, stop in TILES:
                basis[start:stop, :] = dot_t(sketch_rows(start, stop), terms)

        @pl.when(jnp.logical_not(later))
        def _():
            for start, stop in TILES:
                basis[start:stop, :] = sketch_rows(start, stop)

        value = basis[:ROWS, :]
        gram_part[...] = dot(value, value, ((0,), (0,)))
        swap_in(gram_part, g_half, 0, 128).start()

        @pl.when(goes_on)
        def _():
            high, low = split(basis[...])
            for i in range(2):
                rows = slice(256 * i, 256 * i + 256)
                piece_of = delta_t[rows, :]
                back_part[rows, :] = dot16(piece_of, high) + dot16(piece_of, low)
            swap_in(back_part, p_half, 1, 256).start()

        swap_in(gram_part, g_half, 0, 128).wait()
        g_half[...] = g_half[...] + gram_part[rows_of(core, 128), :]
        g_in[chip] = g_half[rows_of(chip, 8), :]
        others(lambda d: scatter_copy(*g_scatter, d).start())

        @pl.when(goes_on)
        def _():
            swap_in(back_part, p_half, 1, 256).wait()
            p_half[...] = p_half[...] + back_part[rows_of(core, 256), :]
            p_in[chip] = p_half[rows_of(chip, 16), :]
            others(lambda d: scatter_copy(*p_scatter, d).start())

        @pl.when(jnp.logical_not(goes_on))
        def _():
            w_out[...] = math.sqrt(D) * dot_t(feature[...], split(inv[...]))

        for item in RS_MESSAGES:
            rs_copy(*item).wait_send()
        for item in AG_MESSAGES:
            ag_copy(*item).wait_send()
        others(lambda d: scatter_landing(*g_scatter, d).wait_recv())
        mine = total(g_in)
        g_own[...] = mine
        gram[rows_of(core * NC + chip, 8), :] = mine
        others(lambda d: gather_copy(*g_gather, d).start())

        @pl.when(goes_on)
        def _():
            others(lambda d: scatter_landing(*p_scatter, d).wait_recv())
            mine = total(p_in)
            p_own[...] = mine
            back[rows_of(core * NC + chip, 16), :] = mine
            others(lambda d: gather_copy(*p_gather, d).start())

        others(lambda d: gather_landing(*g_gather, d).wait_recv())
        swap_out(gram, 3, 128).start()
        swap_landing(gram, 3, 128).wait_recv()
        swap_out(gram, 3, 128).wait_send()
        others(lambda d: scatter_copy(*g_scatter, d).wait_send())
        others(lambda d: gather_copy(*g_gather, d).wait_send())
        work[...] = gram[...]
        factor_panel(work, upper, 0)

        @pl.when(goes_on)
        def _():
            others(lambda d: gather_landing(*p_gather, d).wait_recv())
            swap_out(back, 4, 256).start()
            others(lambda d: scatter_copy(*p_scatter, d).wait_send())
            others(lambda d: gather_copy(*p_gather, d).wait_send())

        factor_panel(work, upper, 1)

        @pl.when(goes_on)
        def _():
            swap_landing(back, 4, 256).wait_recv()
            swap_out(back, 4, 256).wait_send()
            sketch(split(back[...] * (1.0 / norm(gram))))

        return 0

    lax.fori_loop(0, POWER + 1, iteration, 0)

    for k in range(2, R // PANEL):
        factor_panel(work, upper, k)

    last = split(lower_inverse(work))
    at = lax.broadcasted_iota(jnp.int32, (R, R), 0)
    to = lax.broadcasted_iota(jnp.int32, (R, R), 1)
    core_out[...] = jnp.where(at <= to, upper[...], 0.0)
    height = q_out.shape[0]
    for start in range(0, height, 256):
        stop = min(start + 256, height)
        rows = dot_t(basis[start : start + 256, :], last)
        q_out[start:stop, :] = math.sqrt(FF) * rows[: stop - start, :]


def local(delta, probe):
    row_count = delta.shape[0]
    vmem = pl.BlockSpec(memory_space=pltpu.VMEM)

    def floats(*shape):
        return pltpu.VMEM(shape, F32)

    def sems(count):
        return pltpu.SemaphoreType.DMA((count,))

    return pl.pallas_call(
        kernel,
        out_shape=(
            jax.ShapeDtypeStruct((row_count, R), F32),
            jax.ShapeDtypeStruct((COLS, R), F32),
            jax.ShapeDtypeStruct((R, R), F32),
        ),
        in_specs=[vmem] * 2,
        out_specs=(vmem,) * 3,
        scratch_shapes=[
            pltpu.VMEM((COLS, WIDE), BF16),
            floats(NZ * CH, LANES),
            floats(NZ * CH, LANES),
            floats(len(RS_MESSAGES), PARTS[0][1], LANES),
            floats(WIDE, R),
            floats(COLS, R),
            floats(COLS, R),
            floats(COLS, R),
            floats(R, R),
            floats(R, R),
            floats(R, R),
            floats(R, R),
            floats(R, R),
            floats(R, R),
            floats(R, R),
            floats(NZ, 8, R),
            floats(8, R),
            floats(128, R),
            floats(NC, 8, R),
            floats(8, R),
            floats(256, R),
            floats(NC, 16, R),
            floats(16, R),
        ]
        + [sems(len(RS_MESSAGES))] * 2
        + [sems(len(AG_MESSAGES))] * 2
        + [sems(16)] * 2
        + [sems(5)] * 2
        + [sems(16)] * 10,
        compiler_params=pltpu.CompilerParams(
            collective_id=0, has_side_effects=True, vmem_limit_bytes=48 << 20
        ),
        cost_estimate=pl.CostEstimate(flops=10**10, bytes_accessed=10**7, transcendentals=0),
        name="range_finder",
    )(delta, probe)


def solution(mesh):
    in_specs = (P("row", "col"), P("col", None))
    out_specs = (P("row", None), P("col", None), P())
    return jax.shard_map(local, mesh=mesh, in_specs=in_specs, out_specs=out_specs, check_vma=False)
```
